512 devices in a mesh: slab: 128 (over x_lo, z, y), chan: 4 (over x_hi, core).
Axes of the slice: x: 4 (x_hi: 2, x_lo: 2; x = x_hi * 2 + x_lo), y: 8, z: 8, core: 2. Of those that a mesh axis runs over, the one named last changes fastest.
Arguments:
- field_rows: bfloat16 [4, 512, 256, 512], P('chan', None, 'slab'), may hold values from -6 to 6
- region: int32 [128, 64], P('slab', 'chan'), may hold values 0 or 1
- first_kernel: bfloat16 [32, 4, 3, 3, 3], replicated, may hold values from -0.625 to 0.625
- first_bias: float32 [32], replicated, may hold values from -3 to 3
- second_kernel: bfloat16 [128, 32, 3, 3, 3], replicated, may hold values from -0.21875 to 0.21875
Outputs:
- latent: bfloat16 [128, 128, 64, 128], P('chan', 'slab')
The draws below stay inside these ranges and needn't reach their ends.
All inputs are finite; a program needn't handle non-finite values. No bound on the sum of `region` on one device may be relied on, other than what follows from the above.
Results may differ from the reference program's by a relative error of at most 0.013.
Values may be sent and summed in bfloat16 or wider, within the bound.
No kernel may reach another device: no remote copies, remote signals or barrier semaphores. Data moves between devices by JAX's collectives and lax.ppermute only.
A program may use at most 128 MiB of HBM per device.

```python
import jax
import jax.numpy as jnp
from jax import lax

C_IN = 4
C_MID = 32
C_OUT = 128
NX = 512
NZ = 512
NY = 256
N_SLAB = 128
N_CHAN = 4


def place_ends(values, key, low, high):
    longest = values.shape.index(max(values.shape))
    spots = []
    for shift in (0, 1):
        where = [jax.random.randint(jax.random.fold_in(key, axis), (), 0, length) for axis, length in enumerate(values.shape)]
        where[longest] = (where[longest] + shift) % values.shape[longest]
        spots.append(tuple(where))
    return values.at[spots[0]].set(low).at[spots[1]].set(high)


def shard_levels(rng, dims, pieces, smallest, top_value):
    def one(position, shards_of):
        steps = jax.random.uniform(jax.random.fold_in(jax.random.fold_in(rng, 6), position), (shards_of,), jnp.float32, smallest / len(pieces), top_value / len(pieces))
        return jnp.repeat(jnp.exp(steps), dims[position] // shards_of).reshape((-1,) + (1,) * (len(dims) - position - 1))

    level = one(*pieces[0])
    for cut in pieces[1:]:
        level = level * one(*cut)
    return level


def bell_draw(key, shape, scale, reach, shards=(), kind=jnp.bfloat16):
    values = scale * jax.random.normal(key, shape, jnp.float32)
    if shards:
        values = values * shard_levels(key, shape, shards, -0.22, 0.18)
    return jnp.clip(values, -reach, reach).astype(kind)


def setup_inputs(seed: int = 0) -> dict:
    key_list = jax.random.split(jax.random.key(seed), 6)
    field_rows = bell_draw(key_list[0], (C_IN, NZ, NY, NX), 1.0, 6.0, ((0, 4), (2, 128)))
    region = place_ends((jax.random.randint(key_list[1], (NZ // 4, NY // 4), 0, 4) < 3).astype(jnp.int32), jax.random.fold_in(key_list[1], 1), 0, 1)
    first_kernel = bell_draw(key_list[2], (C_MID, C_IN, 3, 3, 3), (C_IN * 27) ** -0.5, 0.625)
    first_bias = bell_draw(key_list[3], (C_MID,), 0.5, 3.0, (), jnp.float32)
    second_kernel = bell_draw(key_list[4], (C_OUT, C_MID, 3, 3, 3), (C_MID * 27) ** -0.5, 0.21875)
    return dict(field_rows=field_rows, region=region, first_kernel=first_kernel, first_bias=first_bias, second_kernel=second_kernel)


def strided_blocks(source, kernel, blocks, groups, finish):
    padded = jnp.pad(source, ((0, 0), (1, 0), (0, 0), (0, 0)))
    per = source.shape[1] // (2 * blocks)
    weights = kernel.astype(jnp.float32)

    def one_block(index):
        start = (index * 2 * per).astype(jnp.int32)
        piece = lax.dynamic_slice_in_dim(padded, start, 2 * per + 1, 1).astype(jnp.float32)
        result = lax.conv_general_dilated(piece[None], weights, (2, 2, 2), ((0, 0), (1, 1), (1, 1)), dimension_numbers=("NCDHW", "OIDHW", "NCDHW"), feature_group_count=groups, precision=lax.Precision.HIGHEST)[0]
        return finish(result)

    stacked = lax.map(one_block, jnp.arange(blocks, dtype=jnp.int32))
    moved = jnp.moveaxis(stacked, 0, 1)
    return moved.reshape((moved.shape[0], blocks * per) + moved.shape[3:])


def reference(field_rows, region, first_kernel, first_bias, second_kernel):
    cover = jnp.repeat(jnp.repeat(region, 4, 0), 4, 1).astype(jnp.bfloat16)
    masked = field_rows * cover[None, :, :, None]

    def first_finish(result):
        return jax.nn.silu(result + first_bias[:, None, None, None]).astype(jnp.bfloat16)

    hidden = strided_blocks(masked, first_kernel, N_SLAB, 1, first_finish)
    width = C_MID // N_CHAN
    grouped = second_kernel.reshape((C_OUT, N_CHAN, width, 3, 3, 3)).transpose(1, 0, 2, 3, 4, 5).reshape((N_CHAN * C_OUT, width, 3, 3, 3))

    def second_finish(result):
        parts = result.reshape((N_CHAN, C_OUT) + result.shape[1:]).astype(jnp.bfloat16)
        parts = lax.optimization_barrier(parts).astype(jnp.float32)
        return jnp.sum(parts, 0).astype(jnp.bfloat16)

    return strided_blocks(hidden, grouped, N_SLAB, N_CHAN, second_finish)
```

```python
import functools

import jax
import jax.numpy as jnp
import numpy as np
from jax import lax
from jax.experimental import pallas as pl
from jax.experimental.pallas import tpu as pltpu
from jax.sharding import Mesh, PartitionSpec as P

FINE = ("x_lo", "z_hi", "z_lo", "y", "x_hi", "core")
SHAPE = (2, 2, 4, 8, 2, 2)
REGION = ("z_lo", "y", "x_hi", "core")
BF = jnp.bfloat16
F32 = jnp.float32


def encoder(block, slab):
    x_lo, z_hi, z_lo, y = slab >> 6, (slab >> 5) & 1, (slab >> 3) & 3, slab & 7
    return (((block * 4 + z_lo) * 8 + y) * 2 + x_lo) * 2 + z_hi


PAIRS = [(b, s) for b in range(4) for s in range(128)]
REGION_ROUTE = [(s * 4 + b, encoder(b, s)) for b, s in PAIRS]
Z_ROUTE = [(encoder(b, s), encoder(b, s + 1)) for b, s in PAIRS if s < 127]
Y_ROUTE = [(encoder(b, s), encoder(b + 1, s)) for b, s in PAIRS if b < 3]
ZY_ROUTE = [(encoder(b, s), encoder(b + 1, s + 1)) for b, s in PAIRS if b < 3 and s < 127]
OUT_ROUTES = [[(encoder(b, s), s * 4 + (b ^ i)) for b, s in PAIRS] for i in range(4)]


def one_hots():
    phases = np.zeros((512, 512), np.float32)
    for x in range(512):
        phases[x, (x % 4) * 128 + x // 4] = 1
    shift = np.zeros((128, 128), np.float32)
    for q in range(127):
        shift[q, q + 1] = 1
    upper = np.zeros((48, 64), np.float32)
    for group in range(8):
        for row in range(6):
            upper[group * 6 + row, group * 8 + 2 + row] = 1
    own = np.zeros((2, 2, 2, 3, 3, 3, 4, 5, 3, 4, 4, 2), np.float32)
    halo = np.zeros((2, 2, 2, 3, 3, 3, 4, 5, 4, 4, 3, 2), np.float32)
    for n in range(2):
        for par in range(2):
            for ky in range(3):
                t, yy = (n, 1) if ky == 0 else (n + 1, ky - 1)
                for kx in range(3):
                    r = 2 * par + kx
                    for c in range(4):
                        for plane, kz, z in ((0, 1, 0), (0, 2, 1), (1, 0, 1), (1, 1, 2), (1, 2, 3)):
                            own[plane, n, par, kz, ky, kx, c, r, t, c, z, yy] = 1
                        for plane, kz, z in ((0, 0, 1), (0, 1, 2), (0, 2, 3), (1, 0, 3)):
                            halo[plane, n, par, kz, ky, kx, c, r, t, c, z - 1, yy] = 1
    return phases, shift, upper, own.reshape(8, 108, 480), halo.reshape(8, 108, 480)


def dot(a, b):
    return jnp.dot(a, b, preferred_element_type=F32)


def split_phases(field_ref, phases_ref, out_ref):
    rows = field_ref[...]
    out_ref[...] = dot(rows, phases_ref[...]).astype(BF).reshape(32, 1, 8, 512)


def mask_rows(region_ref, rows_ref, upper_ref, masked_ref, halo_ref):
    for pair in range(16):
        keep = region_ref[0, pair].astype(F32).astype(BF)
        rows = rows_ref[64 * pair : 64 * pair + 64, :] * keep
        masked_ref[64 * pair : 64 * pair + 64, :] = rows
        halo_ref[48 * pair : 48 * pair + 48, :] = dot(upper_ref[...], rows).astype(BF)


def encode(place_ref, own_ref, zed_ref, why_ref, both_ref, own_kernel_ref, halo_kernel_ref, bias_ref, second_ref, shift_ref, out_ref, own_first, zed_first, hidden, latent):
    block, slab = place_ref[0], place_ref[1]
    shift = shift_ref[...]
    own_first[0:64, :] = dot(why_ref[:, 384:512], shift).astype(BF)
    own_first[64:1088, :] = dot(own_ref[:, 384:512], shift).astype(BF)
    zed_first[0:48, :] = dot(both_ref[:, 384:512], shift).astype(BF)
    zed_first[48:816, :] = dot(zed_ref[:, 384:512], shift).astype(BF)
    bias = bias_ref[...]
    low_plane = jnp.where(slab == 0, 0.0, 1.0).astype(F32)
    low_row = jnp.where(block == 0, 0.0, 1.0).astype(F32)

    def silu(v):
        half = 0.5 * (v + bias)
        return half + half * jnp.tanh(half)

    def operand(first, edge_ref, rows_ref, edge, start, stop):
        pieces = [first[start:stop, :]]
        for r in range(4):
            lanes = slice(128 * r, 128 * r + 128)
            if start < edge:
                pieces += [edge_ref[start:edge, lanes], rows_ref[0 : stop - edge, lanes]]
            else:
                pieces.append(rows_ref[start - edge : stop - edge, lanes])
        return jnp.concatenate(pieces, 0)

    for p in range(17):
        if p < 16:
            own = operand(own_first, why_ref, own_ref, 64, 64 * p, 64 * p + 96)
            zed = operand(zed_first, both_ref, zed_ref, 48, 48 * p, 48 * p + 96)
            upper = dot(own_kernel_ref[...], own)
            lower = dot(halo_kernel_ref[...], zed)
            planes = (lower[0:128], upper[0:128] + lower[128:256], upper[128:256])
        else:
            own = operand(own_first, why_ref, own_ref, 64, 1024, 1088)
            zed = operand(zed_first, both_ref, zed_ref, 48, 768, 816)
            own_w = jnp.concatenate([own_kernel_ref[:, 96 * r : 96 * r + 64] for r in range(5)], 1)
            zed_w = jnp.concatenate([halo_kernel_ref[:, 96 * r : 96 * r + 48] for r in range(5)], 1)
            upper = dot(own_w, own)
            lower = dot(zed_w, zed)
            planes = (lower[0:64], upper[0:64] + lower[128:192], upper[128:192])
        for kz, plane in enumerate(planes):
            rows = plane.shape[0]
            half = 0.5 * (plane + bias[0:rows])
            value = half + half * jnp.tanh(half)
            if kz == 0:
                value = value * low_plane
            if p == 0:
                value = jnp.concatenate([value[0:64] * low_row, value[64:128]], 0)
            hidden[kz, 128 * p : 128 * p + rows, :] = value.astype(BF)

    lane = lax.broadcasted_iota(jnp.int32, (128, 128), 1)
    for o in range(16):
        taps = jnp.concatenate([hidden[kz, 128 * o : 128 * o + 192, :] for kz in range(3)], 0)
        both = dot(second_ref[...], taps)
        earlier = jnp.where(lane == 0, 0.0, pltpu.roll(both[128:256], 1, 1))
        latent[:, o, :] = both[0:128] + earlier
    for g in range(4):
        out_ref[block ^ g] = latent[32 * g : 32 * g + 32].astype(BF)


def join_blocks(place_ref, a_ref, b_ref, c_ref, d_ref, out_ref):
    group = place_ref[0]
    for i, ref in enumerate((a_ref, b_ref, c_ref, d_ref)):
        start = pl.multiple_of((group ^ i) * 16, 16)
        out_ref[:, pl.ds(start, 16), :] = ref[...]


VMEM = pl.BlockSpec(memory_space=pltpu.VMEM)
SMEM = pl.BlockSpec(memory_space=pltpu.SMEM)
PARAMS = pltpu.CompilerParams(vmem_limit_bytes=32 * 1024 * 1024)


def body(field_rows, region, first_kernel, first_bias, second_kernel):
    phases, shift, upper, own_hot, halo_hot = (jnp.asarray(a, BF) for a in one_hots())
    block = lax.axis_index("x_lo") * 2 + lax.axis_index("z_hi")
    inner = lax.axis_index("x_hi") * 2 + lax.axis_index("core")
    slab = inner * 32 + lax.axis_index("z_lo") * 8 + lax.axis_index("y")
    place = jnp.stack([block, slab]).astype(jnp.int32)

    keep = lax.ppermute(region, FINE, REGION_ROUTE)
    split = pl.pallas_call(
        split_phases,
        grid=(4,),
        in_specs=[pl.BlockSpec((256, 512), lambda i: (i, 0)), pl.BlockSpec((512, 512), lambda i: (0, 0))],
        out_specs=pl.BlockSpec((32, 1, 8, 512), lambda i: (0, i, 0, 0)),
        out_shape=jax.ShapeDtypeStruct((32, 4, 8, 512), BF),
        compiler_params=PARAMS,
    )(field_rows.reshape(1024, 512), phases)
    rows = lax.all_to_all(split.reshape(128, 8, 512), REGION, split_axis=0, concat_axis=0, tiled=True)
    own, upper_rows = pl.pallas_call(
        mask_rows,
        in_specs=[SMEM, VMEM, VMEM],
        out_specs=[VMEM, VMEM],
        out_shape=[jax.ShapeDtypeStruct((1024, 512), BF), jax.ShapeDtypeStruct((768, 512), BF)],
        compiler_params=PARAMS,
    )(keep, rows.reshape(1024, 512), upper)
    zed = lax.ppermute(upper_rows, FINE, Z_ROUTE)
    why = lax.ppermute(own[960:1024], FINE, Y_ROUTE)
    both = lax.ppermute(upper_rows[720:768], FINE, ZY_ROUTE)

    taps = first_kernel.transpose(2, 3, 4, 1, 0).reshape(108, 32)
    own_kernel = jnp.einsum("kh,bkm->bhm", taps, own_hot, preferred_element_type=F32).astype(BF).reshape(256, 480)
    halo_kernel = jnp.einsum("kh,bkm->bhm", taps, halo_hot, preferred_element_type=F32).astype(BF).reshape(256, 480)
    bias = jnp.broadcast_to(jnp.tile(first_bias, 4)[:, None], (128, 128))
    second = second_kernel.transpose(0, 2, 3, 4, 1).reshape(128, 9, 3, 32)
    straight = second[:, :, 1:3].reshape(128, 576)
    earlier = jnp.pad(second[:, :, 0:1], ((0, 0), (0, 0), (1, 0), (0, 0))).reshape(128, 576)
    second = jnp.concatenate([straight, earlier], 0)

    pieces = pl.pallas_call(
        encode,
        in_specs=[SMEM] + [VMEM] * 9,
        out_specs=VMEM,
        out_shape=jax.ShapeDtypeStruct((4, 32, 16, 128), BF),
        scratch_shapes=[
            pltpu.VMEM((1088, 128), BF),
            pltpu.VMEM((816, 128), BF),
            pltpu.VMEM((3, 2112, 128), BF),
            pltpu.VMEM((128, 16, 128), F32),
        ],
        compiler_params=PARAMS,
    )(place, own, zed, why, both, own_kernel, halo_kernel, bias, second, shift)
    moved = [lax.ppermute(pieces[i], FINE, OUT_ROUTES[i]) for i in range(4)]
    joined = pl.pallas_call(
        join_blocks,
        in_specs=[SMEM] + [VMEM] * 4,
        out_specs=VMEM,
        out_shape=jax.ShapeDtypeStruct((32, 64, 128), BF),
        compiler_params=PARAMS,
    )(inner.astype(jnp.int32).reshape(1), *moved)
    return joined.reshape(32, 1, 64, 128)


def solution(mesh):
    fine = Mesh(mesh.devices.reshape(SHAPE), FINE)
    slab, chan = FINE[:4], FINE[4:]
    in_specs = (P(chan, None, slab, None), P(slab, chan), P(), P(), P())
    out_specs = P(chan, slab, None, None)
    return jax.shard_map(body, mesh=fine, in_specs=in_specs, out_specs=out_specs, check_vma=False)
```

```python
import functools

import jax
import jax.numpy as jnp
import numpy as np
from jax import lax
from jax.experimental import pallas as pl
from jax.experimental.pallas import tpu as pltpu
from jax.sharding import Mesh, PartitionSpec as P

FINE = ("x_lo", "z_hi", "z_lo", "y", "x_hi", "core")
SHAPE = (2, 2, 4, 8, 2, 2)
REGION = ("z_lo", "y", "x_hi", "core")
BF = jnp.bfloat16
F32 = jnp.float32


MIRROR_Y = True


def encoder(block, slab):
    x_lo, z_hi, z_lo, y = slab >> 6, (slab >> 5) & 1, (slab >> 3) & 3, slab & 7
    z_lo ^= 3 * (z_hi ^ (block & 1))
    y ^= 7 * z_hi * MIRROR_Y
    return (((block * 4 + z_lo) * 8 + y) * 2 + x_lo) * 2 + z_hi


PAIRS = [(b, s) for b in range(4) for s in range(128)]
REGION_ROUTE = [(s * 4 + b, encoder(b, s)) for b, s in PAIRS]
Z_ROUTE = [(encoder(b, s), encoder(b, s + 1)) for b, s in PAIRS if s < 127]
ZY_ROUTE = [(encoder(b, s), encoder(b + 1, s + 1)) for b, s in PAIRS if b < 3 and s < 127]
Y_ROUTE = [(encoder(b, s), encoder(b + 1, s)) for b, s in PAIRS if b < 3]
OUT_ROUTES = [[(encoder(b, s), s * 4 + (b ^ i)) for b, s in PAIRS] for i in range(4)]


def one_hots():
    own = np.zeros((2, 2, 2, 3, 3, 3, 4, 5, 3, 4, 4, 2), np.float32)
    halo = np.zeros((2, 2, 2, 3, 3, 3, 4, 5, 4, 4, 3, 2), np.float32)
    for n in range(2):
        for par in range(2):
            for ky in range(3):
                t, yy = (n, 1) if ky == 0 else (n + 1, ky - 1)
                for kx in range(3):
                    r = 2 * par + kx
                    for c in range(4):
                        for plane, kz, z in ((0, 1, 0), (0, 2, 1), (1, 0, 1), (1, 1, 2), (1, 2, 3)):
                            own[plane, n, par, kz, ky, kx, c, r, t, c, z, yy] = 1
                        for plane, kz, z in ((0, 0, 1), (0, 1, 2), (0, 2, 3), (1, 0, 3)):
                            halo[plane, n, par, kz, ky, kx, c, r, t, c, z - 1, yy] = 1
    return own.reshape(8, 108, 480), halo.reshape(8, 108, 480)


def dot(a, b):
    return jnp.dot(a, b, preferred_element_type=F32)


def one_hot(rows, columns, hit):
    row = lax.broadcasted_iota(jnp.int32, (rows, columns), 0)
    column = lax.broadcasted_iota(jnp.int32, (rows, columns), 1)
    return jnp.where(hit(row, column), 1.0, 0.0).astype(BF)


def next_cell():
    return one_hot(128, 128, lambda q, to: q + 1 == to)


def split_phases(place_ref, field_ref, out_ref, phases_ref):
    @pl.when(pl.program_id(0) == 0)
    def _():
        phases_ref[...] = one_hot(512, 512, lambda x, to: x == 4 * (to & 127) + (to >> 7))

    core = pl.program_id(0) & 1
    flips = 24 * (core ^ (place_ref[0] & 1)) + 7 * core * MIRROR_Y
    rows = dot(field_ref[...].reshape(256, 512), phases_ref[...])
    for k in range(32):
        out_ref[k ^ flips, 0] = rows[8 * k : 8 * k + 8].astype(BF)


def mask_rows(region_ref, rows_ref, masked_ref, halo_ref):
    upper = one_hot(48, 64, lambda row, source: source == row + 2 * ((row * 43) >> 8) + 2)
    for pair in range(16):
        keep = region_ref[0, pair].astype(F32).astype(BF)
        rows = rows_ref[64 * pair : 64 * pair + 64, :] * keep
        masked_ref[64 * pair : 64 * pair + 64, :] = rows
        halo_ref[48 * pair : 48 * pair + 48, :] = dot(upper, rows).astype(BF)


def operand(first, parts):
    return jnp.concatenate([first] + [part[:, 128 * r : 128 * r + 128] for r in range(4) for part in parts], 0)


def silu(v):
    half = 0.5 * v
    return half + half * jnp.tanh(half)


def hidden_planes(lower, upper, rows, bias, low_plane):
    planes = (lower[0:rows], upper[0:rows] + lower[128 : 128 + rows], upper[128 : 128 + rows])
    values = [silu(plane + bias[0:rows]) for plane in planes]
    return [values[0] * low_plane] + values[1:]


def latent_row(second_ref, taps):
    both = dot(second_ref[...], taps)
    lane = lax.broadcasted_iota(jnp.int32, (128, 128), 1)
    return both[0:128] + jnp.where(lane == 0, 0.0, pltpu.roll(both[128:256], 1, 1))


def encode(place_ref, own_ref, zed_ref, why_ref, both_ref, own_kernel_ref, halo_kernel_ref, bias_ref, second_ref, out_ref, own_first, zed_first, hidden, latent):
    block, slab = place_ref[0], place_ref[1]
    shift = next_cell()
    own_first[0:64, :] = dot(why_ref[:, 384:512], shift).astype(BF)
    own_first[64:1088, :] = dot(own_ref[:, 384:512], shift).astype(BF)
    zed_first[0:48, :] = dot(both_ref[:, 384:512], shift).astype(BF)
    zed_first[48:816, :] = dot(zed_ref[:, 384:512], shift).astype(BF)
    bias = bias_ref[...]
    low_plane = jnp.where(slab == 0, 0.0, 1.0).astype(F32)
    low_row = jnp.where(block == 0, 0.0, 1.0).astype(F32)
    for p in range(17):
        rows, own_rows, zed_rows = 128, 96, 96
        own_w, zed_w = own_kernel_ref[...], halo_kernel_ref[...]
        if p == 16:
            rows, own_rows, zed_rows = 64, 64, 48
            own_w = jnp.concatenate([own_w[:, 96 * r : 96 * r + 64] for r in range(5)], 1)
            zed_w = jnp.concatenate([zed_w[:, 96 * r : 96 * r + 48] for r in range(5)], 1)
        if p == 0:
            own_parts, zed_parts = [why_ref[...], own_ref[0:32, :]], [both_ref[...], zed_ref[0:48, :]]
        else:
            own_parts = [own_ref[64 * p - 64 : 64 * p - 64 + own_rows, :]]
            zed_parts = [zed_ref[48 * p - 48 : 48 * p - 48 + zed_rows, :]]
        upper = dot(own_w, operand(own_first[64 * p : 64 * p + own_rows, :], own_parts))
        lower = dot(zed_w, operand(zed_first[48 * p : 48 * p + zed_rows, :], zed_parts))
        for kz, value in enumerate(hidden_planes(lower, upper, rows, bias, low_plane)):
            if p == 0:
                value = jnp.concatenate([value[0:64] * low_row, value[64:128]], 0)
            hidden[kz, 128 * p : 128 * p + rows, :] = value.astype(BF)
    for o in range(16):
        taps = jnp.concatenate([hidden[kz, 128 * o : 128 * o + 192, :] for kz in range(3)], 0)
        latent[:, o, :] = latent_row(second_ref, taps)
    for g in range(4):
        out_ref[block ^ g] = latent[32 * g : 32 * g + 32].astype(BF)


def join_blocks(place_ref, a_ref, b_ref, c_ref, d_ref, out_ref):
    group = place_ref[0]
    for i, ref in enumerate((a_ref, b_ref, c_ref, d_ref)):
        start = pl.multiple_of((group ^ i) * 16, 16)
        out_ref[:, pl.ds(start, 16), :] = ref[...]


VMEM = pl.BlockSpec(memory_space=pltpu.VMEM)
SMEM = pl.BlockSpec(memory_space=pltpu.SMEM)
PARAMS = pltpu.CompilerParams(vmem_limit_bytes=32 * 1024 * 1024)


def body(field_rows, region, first_kernel, first_bias, second_kernel):
    own_hot, halo_hot = (jnp.asarray(a, BF) for a in one_hots())
    block = lax.axis_index("x_lo") * 2 + lax.axis_index("z_hi")
    inner = lax.axis_index("x_hi") * 2 + lax.axis_index("core")
    core = lax.axis_index("core")
    z_lo = lax.axis_index("z_lo") ^ (3 * (core ^ lax.axis_index("z_hi")))
    slab = inner * 32 + z_lo * 8 + (lax.axis_index("y") ^ (7 * core * MIRROR_Y))
    place = jnp.stack([block, slab]).astype(jnp.int32)

    keep = lax.ppermute(region, FINE, REGION_ROUTE)
    split = pl.pallas_call(
        split_phases,
        grid=(4,),
        in_specs=[SMEM, pl.BlockSpec((128, 2, 512), lambda i: (i, 0, 0))],
        out_specs=pl.BlockSpec((32, 1, 8, 512), lambda i: (0, i, 0, 0)),
        out_shape=jax.ShapeDtypeStruct((32, 4, 8, 512), BF),
        scratch_shapes=[pltpu.VMEM((512, 512), BF)],
        compiler_params=pltpu.CompilerParams(vmem_limit_bytes=60 * 1024 * 1024),
    )(place, field_rows.reshape(512, 2, 512))
    rows = lax.all_to_all(split.reshape(128, 8, 512), REGION, split_axis=0, concat_axis=0, tiled=True)
    taps = first_kernel.transpose(2, 3, 4, 1, 0).reshape(108, 32)
    own_kernel = jnp.einsum("kh,bkm->bhm", taps, own_hot, preferred_element_type=F32).astype(BF).reshape(256, 480)
    halo_kernel = jnp.einsum("kh,bkm->bhm", taps, halo_hot, preferred_element_type=F32).astype(BF).reshape(256, 480)
    bias = jnp.broadcast_to(jnp.tile(first_bias, 4)[:, None], (128, 128))
    second = second_kernel.transpose(0, 2, 3, 4, 1).reshape(128, 9, 3, 32)
    straight = second[:, :, 1:3].reshape(128, 576)
    earlier = jnp.pad(second[:, :, 0:1], ((0, 0), (0, 0), (1, 0), (0, 0))).reshape(128, 576)
    second = jnp.concatenate([straight, earlier], 0)

    rows, own_kernel, halo_kernel, bias, second = lax.optimization_barrier((rows, own_kernel, halo_kernel, bias, second))
    own, upper_rows = pl.pallas_call(
        mask_rows,
        in_specs=[SMEM, VMEM],
        out_specs=[VMEM, VMEM],
        out_shape=[jax.ShapeDtypeStruct((1024, 512), BF), jax.ShapeDtypeStruct((768, 512), BF)],
        compiler_params=PARAMS,
    )(keep, rows.reshape(1024, 512))
    zed = lax.ppermute(upper_rows, FINE, Z_ROUTE)
    why = lax.ppermute(own[960:1024], FINE, Y_ROUTE)
    both = lax.ppermute(upper_rows[720:768], FINE, ZY_ROUTE)
    pieces = pl.pallas_call(
        encode,
        in_specs=[SMEM] + [VMEM] * 8,
        out_specs=VMEM,
        out_shape=jax.ShapeDtypeStruct((4, 32, 16, 128), BF),
        scratch_shapes=[
            pltpu.VMEM((1088, 128), BF),
            pltpu.VMEM((816, 128), BF),
            pltpu.VMEM((3, 2112, 128), BF),
            pltpu.VMEM((128, 16, 128), F32),
        ],
        compiler_params=PARAMS,
    )(place, own, zed, why, both, own_kernel, halo_kernel, bias, second)
    moved = [lax.ppermute(pieces[i], FINE, OUT_ROUTES[i]) for i in range(4)]
    joined = pl.pallas_call(
        join_blocks,
        in_specs=[SMEM] + [VMEM] * 4,
        out_specs=VMEM,
        out_shape=jax.ShapeDtypeStruct((32, 64, 128), BF),
        compiler_params=PARAMS,
    )(inner.astype(jnp.int32).reshape(1), *moved)
    return joined.reshape(32, 1, 64, 128)


def solution(mesh):
    fine = Mesh(mesh.devices.reshape(SHAPE), FINE)
    slab, chan = FINE[:4], FINE[4:]
    in_specs = (P(chan, None, slab, None), P(slab, chan), P(), P(), P())
    out_specs = P(chan, slab, None, None)
    return jax.shard_map(body, mesh=fine, in_specs=in_specs, out_specs=out_specs, check_vma=False)
```

```python
import functools

import jax
import jax.numpy as jnp
import numpy as np
from jax import lax
from jax.experimental import pallas as pl
from jax.experimental.pallas import tpu as pltpu
from jax.sharding import Mesh, PartitionSpec as P

FINE = ("x_lo", "z_hi", "z_lo", "y", "x_hi", "core")
SHAPE = (2, 2, 4, 8, 2, 2)
REGION = ("z_lo", "y", "x_hi", "core")
BF = jnp.bfloat16
F32 = jnp.float32


MIRROR_Y = True


def encoder(block, slab):
    x_lo, z_hi, z_lo, y = slab >> 6, (slab >> 5) & 1, (slab >> 3) & 3, slab & 7
    z_lo ^= 3 * (z_hi ^ (block & 1))
    y ^= 7 * z_hi * MIRROR_Y
    return (((block * 4 + z_lo) * 8 + y) * 2 + x_lo) * 2 + z_hi


PAIRS = [(b, s) for b in range(4) for s in range(128)]
REGION_ROUTE = [(s * 4 + b, encoder(b, s)) for b, s in PAIRS]
Z_ROUTE = [(encoder(b, s), encoder(b, s + 1)) for b, s in PAIRS if s < 127]
ZY_ROUTE = [(encoder(b, s), encoder(b + 1, s + 1)) for b, s in PAIRS if b < 3 and s < 127]
Y_ROUTE = [(encoder(b, s), encoder(b + 1, s)) for b, s in PAIRS if b < 3]
OUT_ROUTES = [[(encoder(b, s), s * 4 + (b ^ i)) for b, s in PAIRS] for i in (0, 2)]
CORE_ROUTE = [(i, i ^ 1) for i in range(512)]


def one_hots():
    own = np.zeros((2, 2, 2, 3, 3, 3, 4, 5, 3, 4, 4, 2), np.float32)
    halo = np.zeros((2, 2, 2, 3, 3, 3, 4, 5, 4, 4, 3, 2), np.float32)
    for n in range(2):
        for par in range(2):
            for ky in range(3):
                t, yy = (n, 1) if ky == 0 else (n + 1, ky - 1)
                for kx in range(3):
                    r = 2 * par + kx
                    for c in range(4):
                        for plane, kz, z in ((0, 1, 0), (0, 2, 1), (1, 0, 1), (1, 1, 2), (1, 2, 3)):
                            own[plane, n, par, kz, ky, kx, c, r, t, c, z, yy] = 1
                        for plane, kz, z in ((0, 0, 1), (0, 1, 2), (0, 2, 3), (1, 0, 3)):
                            halo[plane, n, par, kz, ky, kx, c, r, t, c, z - 1, yy] = 1
    return own.reshape(8, 108, 480), halo.reshape(8, 108, 480)


def dot(a, b):
    return jnp.dot(a, b, preferred_element_type=F32)


def one_hot(rows, columns, hit):
    row = lax.broadcasted_iota(jnp.int32, (rows, columns), 0)
    column = lax.broadcasted_iota(jnp.int32, (rows, columns), 1)
    return jnp.where(hit(row, column), 1.0, 0.0).astype(BF)


def next_cell():
    return one_hot(128, 128, lambda q, to: q + 1 == to)


def split_phases(field_ref, out_ref, phases_ref):
    @pl.when(pl.program_id(0) == 0)
    def _():
        phases_ref[...] = one_hot(512, 512, lambda x, to: x == 4 * (to & 127) + (to >> 7))

    core = pl.program_id(0) & 1
    flips = 24 * (core ^ lax.axis_index("z_hi")) + 7 * core * MIRROR_Y
    rows = dot(field_ref[...].reshape(256, 512), phases_ref[...])
    for k in range(32):
        out_ref[k ^ flips, 0] = rows[8 * k : 8 * k + 8].astype(BF)


def mask_rows(region_ref, rows_ref, masked_ref, halo_ref):
    upper = one_hot(48, 64, lambda row, source: source == row + 2 * ((row * 43) >> 8) + 2)
    for pair in range(16):
        keep = region_ref[0, pair].astype(F32).astype(BF)
        rows = rows_ref[64 * pair : 64 * pair + 64, :] * keep
        masked_ref[64 * pair : 64 * pair + 64, :] = rows
        halo_ref[48 * pair : 48 * pair + 48, :] = dot(upper, rows).astype(BF)


def operand(first, parts):
    return jnp.concatenate([first] + [part[:, 128 * r : 128 * r + 128] for r in range(4) for part in parts], 0)


def silu(v):
    half = 0.5 * v
    return half + half * jnp.tanh(half)


def hidden_planes(lower, upper, rows, bias, low_plane):
    planes = (lower[0:rows], upper[0:rows] + lower[128 : 128 + rows], upper[128 : 128 + rows])
    values = [silu(plane + bias[0:rows]) for plane in planes]
    return [values[0] * low_plane] + values[1:]


def latent_row(second_ref, taps):
    both = dot(second_ref[...], taps)
    lane = lax.broadcasted_iota(jnp.int32, (128, 128), 1)
    return both[0:128] + jnp.where(lane == 0, 0.0, pltpu.roll(both[128:256], 1, 1))


def encode(place_ref, own_ref, zed_ref, why_ref, both_ref, own_kernel_ref, halo_kernel_ref, bias_ref, second_ref, out_ref, own_first, zed_first, hidden, latent):
    block, slab = place_ref[0], place_ref[1]
    shift = next_cell()
    own_first[0:64, :] = dot(why_ref[:, 384:512], shift).astype(BF)
    own_first[64:1088, :] = dot(own_ref[:, 384:512], shift).astype(BF)
    zed_first[0:48, :] = dot(both_ref[:, 384:512], shift).astype(BF)
    zed_first[48:816, :] = dot(zed_ref[:, 384:512], shift).astype(BF)
    bias = bias_ref[...]
    low_plane = jnp.where(slab == 0, 0.0, 1.0).astype(F32)
    low_row = jnp.where(block == 0, 0.0, 1.0).astype(F32)
    for p in range(17):
        rows, own_rows, zed_rows = 128, 96, 96
        own_w, zed_w = own_kernel_ref[...], halo_kernel_ref[...]
        if p == 16:
            rows, own_rows, zed_rows = 64, 64, 48
            own_w = jnp.concatenate([own_w[:, 96 * r : 96 * r + 64] for r in range(5)], 1)
            zed_w = jnp.concatenate([zed_w[:, 96 * r : 96 * r + 48] for r in range(5)], 1)
        if p == 0:
            own_parts, zed_parts = [why_ref[...], own_ref[0:32, :]], [both_ref[...], zed_ref[0:48, :]]
        else:
            own_parts = [own_ref[64 * p - 64 : 64 * p - 64 + own_rows, :]]
            zed_parts = [zed_ref[48 * p - 48 : 48 * p - 48 + zed_rows, :]]
        upper = dot(own_w, operand(own_first[64 * p : 64 * p + own_rows, :], own_parts))
        lower = dot(zed_w, operand(zed_first[48 * p : 48 * p + zed_rows, :], zed_parts))
        for kz, value in enumerate(hidden_planes(lower, upper, rows, bias, low_plane)):
            if p == 0:
                value = jnp.concatenate([value[0:64] * low_row, value[64:128]], 0)
            hidden[kz, 128 * p : 128 * p + rows, :] = value.astype(BF)
    for o in range(16):
        taps = jnp.concatenate([hidden[kz, 128 * o : 128 * o + 192, :] for kz in range(3)], 0)
        latent[:, o, :] = latent_row(second_ref, taps)
    for g in range(4):
        out_ref[(block & 2) ^ g] = latent[32 * g : 32 * g + 32].astype(BF)


def join_blocks(place_ref, a_ref, b_ref, other_ref, out_ref):
    group = place_ref[0]
    core = group & 1
    for i, ref in enumerate((a_ref, b_ref)):
        near = pl.multiple_of((group ^ (2 * i)) * 16, 16)
        out_ref[:, pl.ds(near, 16), :] = ref[core]
        far = pl.multiple_of((group ^ (2 * i + 1)) * 16, 16)
        out_ref[:, pl.ds(far, 16), :] = other_ref[i]


VMEM = pl.BlockSpec(memory_space=pltpu.VMEM)
SMEM = pl.BlockSpec(memory_space=pltpu.SMEM)
PARAMS = pltpu.CompilerParams(vmem_limit_bytes=32 * 1024 * 1024)


def body(field_rows, region, first_kernel, first_bias, second_kernel):
    own_hot, halo_hot = (jnp.asarray(a, BF) for a in one_hots())
    block = lax.axis_index("x_lo") * 2 + lax.axis_index("z_hi")
    inner = lax.axis_index("x_hi") * 2 + lax.axis_index("core")
    core = lax.axis_index("core")
    z_lo = lax.axis_index("z_lo") ^ (3 * (core ^ lax.axis_index("z_hi")))
    slab = inner * 32 + z_lo * 8 + (lax.axis_index("y") ^ (7 * core * MIRROR_Y))
    place = jnp.stack([block, slab]).astype(jnp.int32)

    keep = lax.ppermute(region, FINE, REGION_ROUTE)
    split = pl.pallas_call(
        split_phases,
        grid=(4,),
        in_specs=[pl.BlockSpec((128, 2, 512), lambda i: (i, 0, 0))],
        out_specs=pl.BlockSpec((32, 1, 8, 512), lambda i: (0, i, 0, 0)),
        out_shape=jax.ShapeDtypeStruct((32, 4, 8, 512), BF),
        scratch_shapes=[pltpu.VMEM((512, 512), BF)],
        compiler_params=pltpu.CompilerParams(vmem_limit_bytes=60 * 1024 * 1024),
    )(field_rows.reshape(512, 2, 512))
    rows = lax.all_to_all(split.reshape(128, 8, 512), REGION, split_axis=0, concat_axis=0, tiled=True)
    taps = first_kernel.transpose(2, 3, 4, 1, 0).reshape(108, 32)
    own_kernel = jnp.einsum("kh,bkm->bhm", taps, own_hot, preferred_element_type=F32).astype(BF).reshape(256, 480)
    halo_kernel = jnp.einsum("kh,bkm->bhm", taps, halo_hot, preferred_element_type=F32).astype(BF).reshape(256, 480)
    bias = jnp.broadcast_to(jnp.tile(first_bias, 4)[:, None], (128, 128))
    second = second_kernel.transpose(0, 2, 3, 4, 1).reshape(128, 9, 3, 32)
    straight = second[:, :, 1:3].reshape(128, 576)
    earlier = jnp.pad(second[:, :, 0:1], ((0, 0), (0, 0), (1, 0), (0, 0))).reshape(128, 576)
    second = jnp.concatenate([straight, earlier], 0)

    rows, own_kernel, halo_kernel, bias, second = lax.optimization_barrier((rows, own_kernel, halo_kernel, bias, second))
    own, upper_rows = pl.pallas_call(
        mask_rows,
        in_specs=[SMEM, VMEM],
        out_specs=[VMEM, VMEM],
        out_shape=[jax.ShapeDtypeStruct((1024, 512), BF), jax.ShapeDtypeStruct((768, 512), BF)],
        compiler_params=PARAMS,
    )(keep, rows.reshape(1024, 512))
    zed = lax.ppermute(upper_rows, FINE, Z_ROUTE)
    why = lax.ppermute(own[960:1024], FINE, Y_ROUTE)
    both = lax.ppermute(upper_rows[720:768], FINE, ZY_ROUTE)
    pieces = pl.pallas_call(
        encode,
        in_specs=[SMEM] + [VMEM] * 8,
        out_specs=VMEM,
        out_shape=jax.ShapeDtypeStruct((4, 32, 16, 128), BF),
        scratch_shapes=[
            pltpu.VMEM((1088, 128), BF),
            pltpu.VMEM((816, 128), BF),
            pltpu.VMEM((3, 2112, 128), BF),
            pltpu.VMEM((128, 16, 128), F32),
        ],
        compiler_params=PARAMS,
    )(place, own, zed, why, both, own_kernel, halo_kernel, bias, second)
    a, b = (lax.ppermute(pieces[2 * i : 2 * i + 2], FINE, OUT_ROUTES[i]) for i in range(2))
    away = jnp.stack([lax.dynamic_index_in_dim(v, 1 - core, 0, keepdims=False) for v in (a, b)])
    other = lax.ppermute(away, FINE, CORE_ROUTE)
    joined = pl.pallas_call(
        join_blocks,
        in_specs=[SMEM] + [VMEM] * 3,
        out_specs=VMEM,
        out_shape=jax.ShapeDtypeStruct((32, 64, 128), BF),
        compiler_params=PARAMS,
    )(inner.astype(jnp.int32).reshape(1), a, b, other)
    return joined.reshape(32, 1, 64, 128)


def solution(mesh):
    fine = Mesh(mesh.devices.reshape(SHAPE), FINE)
    slab, chan = FINE[:4], FINE[4:]
    in_specs = (P(chan, None, slab, None), P(slab, chan), P(), P(), P())
    out_specs = P(chan, slab, None, None)
    return jax.shard_map(body, mesh=fine, in_specs=in_specs, out_specs=out_specs, check_vma=False)
```

```python
import functools

import jax
import jax.numpy as jnp
import numpy as np
from jax import lax
from jax.experimental import pallas as pl
from jax.experimental.pallas import tpu as pltpu
from jax.sharding import Mesh, PartitionSpec as P

FINE = ("x_lo", "z_hi", "z_lo", "y", "x_hi", "core")
SHAPE = (2, 2, 4, 8, 2, 2)
REGION = ("z_lo", "y", "x_hi", "core")
BF = jnp.bfloat16
F32 = jnp.float32


MIRROR_Y = True


def encoder(block, slab):
    x_lo, z_hi, z_lo, y = slab >> 6, (slab >> 5) & 1, (slab >> 3) & 3, slab & 7
    z_lo ^= 3 * (z_hi ^ (block & 1))
    y ^= 7 * z_hi * MIRROR_Y
    return (((block * 4 + z_lo) * 8 + y) * 2 + x_lo) * 2 + z_hi


PAIRS = [(b, s) for b in range(4) for s in range(128)]
REGION_ROUTE = [(s * 4 + b, encoder(b, s)) for b, s in PAIRS]
Z_ROUTE = [(encoder(b, s), encoder(b, s + 1)) for b, s in PAIRS if s < 127]
ZY_ROUTE = [(encoder(b, s), encoder(b + 1, s + 1)) for b, s in PAIRS if b < 3 and s < 127]
Y_ROUTE = [(encoder(b, s), encoder(b + 1, s)) for b, s in PAIRS if b < 3]
OUT_ROUTES = [[(encoder(b, s), s * 4 + (b ^ i)) for b, s in PAIRS] for i in (0, 2)]
CORE_ROUTE = [(i, i ^ 1) for i in range(512)]


def one_hots():
    own = np.zeros((2, 2, 2, 3, 3, 3, 4, 5, 3, 4, 4, 2), np.float32)
    halo = np.zeros((2, 2, 2, 3, 3, 3, 4, 5, 4, 4, 3, 2), np.float32)
    for n in range(2):
        for par in range(2):
            for ky in range(3):
                t, yy = (n, 1) if ky == 0 else (n + 1, ky - 1)
                for kx in range(3):
                    r = 2 * par + kx
                    for c in range(4):
                        for plane, kz, z in ((0, 1, 0), (0, 2, 1), (1, 0, 1), (1, 1, 2), (1, 2, 3)):
                            own[plane, n, par, kz, ky, kx, c, r, t, c, z, yy] = 1
                        for plane, kz, z in ((0, 0, 1), (0, 1, 2), (0, 2, 3), (1, 0, 3)):
                            halo[plane, n, par, kz, ky, kx, c, r, t, c, z - 1, yy] = 1
    return own.reshape(8, 108, 480), halo.reshape(8, 108, 480)


def dot(a, b):
    return jnp.dot(a, b, preferred_element_type=F32)


def one_hot(rows, columns, hit):
    row = lax.broadcasted_iota(jnp.int32, (rows, columns), 0)
    column = lax.broadcasted_iota(jnp.int32, (rows, columns), 1)
    return jnp.where(hit(row, column), 1.0, 0.0).astype(BF)


def next_cell():
    return one_hot(128, 128, lambda q, to: q + 1 == to)


def split_phases(field_ref, out_ref, phases_ref):
    @pl.when(pl.program_id(0) == 0)
    def _():
        phases_ref[...] = one_hot(512, 512, lambda x, to: x == 4 * (to & 127) + (to >> 7))

    core = pl.program_id(0) & 1
    flips = 24 * (core ^ lax.axis_index("z_hi")) + 7 * core * MIRROR_Y
    rows = dot(field_ref[...].reshape(256, 512), phases_ref[...])
    for k in range(32):
        out_ref[k ^ flips, 0] = rows[8 * k : 8 * k + 8].astype(BF)


def mask_rows(region_ref, rows_ref, masked_ref, halo_ref, tail_ref, corner_ref):
    upper = one_hot(48, 64, lambda row, source: source == row + 2 * ((row * 43) >> 8) + 2)
    for pair in range(16):
        keep = region_ref[0, pair].astype(F32).astype(BF)
        rows = rows_ref[64 * pair : 64 * pair + 64, :] * keep
        masked_ref[64 * pair : 64 * pair + 64, :] = rows
        upper_rows = dot(upper, rows).astype(BF)
        halo_ref[48 * pair : 48 * pair + 48, :] = upper_rows
    tail_ref[...] = rows
    corner_ref[...] = upper_rows


def operand(first, parts):
    return jnp.concatenate([first] + [part[:, 128 * r : 128 * r + 128] for r in range(4) for part in parts], 0)


def silu(v):
    half = 0.5 * v
    return half + half * jnp.tanh(half)


def hidden_planes(lower, upper, rows, bias, low_plane):
    planes = (lower[0:rows], upper[0:rows] + lower[128 : 128 + rows], upper[128 : 128 + rows])
    values = [silu(plane + bias[0:rows]) for plane in planes]
    return [values[0] * low_plane] + values[1:]


def latent_row(second_ref, taps):
    both = dot(second_ref[...], taps)
    lane = lax.broadcasted_iota(jnp.int32, (128, 128), 1)
    return both[0:128] + jnp.where(lane == 0, 0.0, pltpu.roll(both[128:256], 1, 1))


def encode(place_ref, own_ref, zed_ref, why_ref, both_ref, own_kernel_ref, halo_kernel_ref, bias_ref, second_ref, out_ref, own_first, zed_first, hidden, latent):
    block, slab = place_ref[0], place_ref[1]
    shift = next_cell()
    own_first[0:64, :] = dot(why_ref[:, 384:512], shift).astype(BF)
    own_first[64:1088, :] = dot(own_ref[:, 384:512], shift).astype(BF)
    zed_first[0:48, :] = dot(both_ref[:, 384:512], shift).astype(BF)
    zed_first[48:816, :] = dot(zed_ref[:, 384:512], shift).astype(BF)
    bias = bias_ref[...]
    low_plane = jnp.where(slab == 0, 0.0, 1.0).astype(F32)
    low_row = jnp.where(block == 0, 0.0, 1.0).astype(F32)
    for p in range(17):
        rows, own_rows, zed_rows = 128, 96, 96
        own_w, zed_w = own_kernel_ref[...], halo_kernel_ref[...]
        if p == 16:
            rows, own_rows, zed_rows = 64, 64, 48
            own_w = jnp.concatenate([own_w[:, 96 * r : 96 * r + 64] for r in range(5)], 1)
            zed_w = jnp.concatenate([zed_w[:, 96 * r : 96 * r + 48] for r in range(5)], 1)
        if p == 0:
            own_parts, zed_parts = [why_ref[...], own_ref[0:32, :]], [both_ref[...], zed_ref[0:48, :]]
        else:
            own_parts = [own_ref[64 * p - 64 : 64 * p - 64 + own_rows, :]]
            zed_parts = [zed_ref[48 * p - 48 : 48 * p - 48 + zed_rows, :]]
        upper = dot(own_w, operand(own_first[64 * p : 64 * p + own_rows, :], own_parts))
        lower = dot(zed_w, operand(zed_first[48 * p : 48 * p + zed_rows, :], zed_parts))
        for kz, value in enumerate(hidden_planes(lower, upper, rows, bias, low_plane)):
            if p == 0:
                value = jnp.concatenate([value[0:64] * low_row, value[64:128]], 0)
            hidden[kz, 128 * p : 128 * p + rows, :] = value.astype(BF)
    for o in range(16):
        taps = jnp.concatenate([hidden[kz, 128 * o : 128 * o + 192, :] for kz in range(3)], 0)
        latent[:, o, :] = latent_row(second_ref, taps)
    for g in range(4):
        out_ref[(block & 2) ^ g] = latent[32 * g : 32 * g + 32].astype(BF)


def join_blocks(place_ref, a_ref, b_ref, other_ref, out_ref):
    group = place_ref[0]
    core = group & 1
    for i, ref in enumerate((a_ref, b_ref)):
        near = pl.multiple_of((group ^ (2 * i)) * 16, 16)
        out_ref[:, pl.ds(near, 16), :] = ref[core]
        far = pl.multiple_of((group ^ (2 * i + 1)) * 16, 16)
        out_ref[:, pl.ds(far, 16), :] = other_ref[i]


VMEM = pl.BlockSpec(memory_space=pltpu.VMEM)
SMEM = pl.BlockSpec(memory_space=pltpu.SMEM)
PARAMS = pltpu.CompilerParams(vmem_limit_bytes=32 * 1024 * 1024)


def body(field_rows, region, first_kernel, first_bias, second_kernel):
    own_hot, halo_hot = (jnp.asarray(a, BF) for a in one_hots())
    block = lax.axis_index("x_lo") * 2 + lax.axis_index("z_hi")
    inner = lax.axis_index("x_hi") * 2 + lax.axis_index("core")
    core = lax.axis_index("core")
    z_lo = lax.axis_index("z_lo") ^ (3 * (core ^ lax.axis_index("z_hi")))
    slab = inner * 32 + z_lo * 8 + (lax.axis_index("y") ^ (7 * core * MIRROR_Y))
    place = jnp.stack([block, slab]).astype(jnp.int32)

    keep = lax.ppermute(region, FINE, REGION_ROUTE)
    split = pl.pallas_call(
        split_phases,
        grid=(4,),
        in_specs=[pl.BlockSpec((128, 2, 512), lambda i: (i, 0, 0))],
        out_specs=pl.BlockSpec((32, 1, 8, 512), lambda i: (0, i, 0, 0)),
        out_shape=jax.ShapeDtypeStruct((32, 4, 8, 512), BF),
        scratch_shapes=[pltpu.VMEM((512, 512), BF)],
        compiler_params=pltpu.CompilerParams(vmem_limit_bytes=60 * 1024 * 1024),
    )(field_rows.reshape(512, 2, 512))
    rows = lax.all_to_all(split.reshape(128, 8, 512), REGION, split_axis=0, concat_axis=0, tiled=True)
    taps = first_kernel.transpose(2, 3, 4, 1, 0).reshape(108, 32)
    own_kernel = jnp.einsum("kh,bkm->bhm", taps, own_hot, preferred_element_type=F32).astype(BF).reshape(256, 480)
    halo_kernel = jnp.einsum("kh,bkm->bhm", taps, halo_hot, preferred_element_type=F32).astype(BF).reshape(256, 480)
    bias = jnp.broadcast_to(jnp.tile(first_bias, 4)[:, None], (128, 128))
    second = second_kernel.transpose(0, 2, 3, 4, 1).reshape(128, 9, 3, 32)
    straight = second[:, :, 1:3].reshape(128, 576)
    earlier = jnp.pad(second[:, :, 0:1], ((0, 0), (0, 0), (1, 0), (0, 0))).reshape(128, 576)
    second = jnp.concatenate([straight, earlier], 0)

    rows, own_kernel, halo_kernel, bias, second = lax.optimization_barrier((rows, own_kernel, halo_kernel, bias, second))
    own, upper_rows, tail, corner = pl.pallas_call(
        mask_rows,
        in_specs=[SMEM, VMEM],
        out_specs=[VMEM] * 4,
        out_shape=[jax.ShapeDtypeStruct((n, 512), BF) for n in (1024, 768, 64, 48)],
        compiler_params=PARAMS,
    )(keep, rows.reshape(1024, 512))
    zed = lax.ppermute(upper_rows, FINE, Z_ROUTE)
    why = lax.ppermute(tail, FINE, Y_ROUTE)
    both = lax.ppermute(corner, FINE, ZY_ROUTE)
    pieces = pl.pallas_call(
        encode,
        in_specs=[SMEM] + [VMEM] * 8,
        out_specs=VMEM,
        out_shape=jax.ShapeDtypeStruct((4, 32, 16, 128), BF),
        scratch_shapes=[
            pltpu.VMEM((1088, 128), BF),
            pltpu.VMEM((816, 128), BF),
            pltpu.VMEM((3, 2112, 128), BF),
            pltpu.VMEM((128, 16, 128), F32),
        ],
        compiler_params=PARAMS,
    )(place, own, zed, why, both, own_kernel, halo_kernel, bias, second)
    a, b = (lax.ppermute(pieces[2 * i : 2 * i + 2], FINE, OUT_ROUTES[i]) for i in range(2))
    away = jnp.stack([lax.dynamic_index_in_dim(v, 1 - core, 0, keepdims=False) for v in (a, b)])
    other = lax.ppermute(away, FINE, CORE_ROUTE)
    joined = pl.pallas_call(
        join_blocks,
        in_specs=[SMEM] + [VMEM] * 3,
        out_specs=VMEM,
        out_shape=jax.ShapeDtypeStruct((32, 64, 128), BF),
        compiler_params=PARAMS,
    )(inner.astype(jnp.int32).reshape(1), a, b, other)
    return joined.reshape(32, 1, 64, 128)


def solution(mesh):
    fine = Mesh(mesh.devices.reshape(SHAPE), FINE)
    slab, chan = FINE[:4], FINE[4:]
    in_specs = (P(chan, None, slab, None), P(slab, chan), P(), P(), P())
    out_specs = P(chan, slab, None, None)
    return jax.shard_map(body, mesh=fine, in_specs=in_specs, out_specs=out_specs, check_vma=False)
```

```python
import functools

import jax
import jax.numpy as jnp
import numpy as np
from jax import lax
from jax.experimental import pallas as pl
from jax.experimental.pallas import tpu as pltpu
from jax.sharding import Mesh, PartitionSpec as P

FINE = ("x_lo", "z_hi", "z_lo", "y", "x_hi", "core")
SHAPE = (2, 2, 4, 8, 2, 2)
REGION = ("z_lo", "y", "x_hi", "core")
BF = jnp.bfloat16
F32 = jnp.float32


def encoder(block, slab):
    x_lo, z_hi, z_lo, y = slab >> 6, (slab >> 5) & 1, (slab >> 3) & 3, slab & 7
    y ^= 7 * (z_lo & 1)
    z_lo ^= 3 * (z_hi ^ (block & 1))
    return (((block * 4 + z_lo) * 8 + y) * 2 + x_lo) * 2 + z_hi


PAIRS = [(b, s) for b in range(4) for s in range(128)]
REGION_ROUTE = [(s * 4 + b, encoder(b, s)) for b, s in PAIRS]
Z_ROUTE = [(encoder(b, s), encoder(b, s + 1)) for b, s in PAIRS if s < 127]
ZY_ROUTE = [(encoder(b, s), encoder(b + 1, s + 1)) for b, s in PAIRS if b < 3 and s < 127]
Y_ROUTE = [(encoder(b, s), encoder(b + 1, s)) for b, s in PAIRS if b < 3]
OUT_ROUTES = [[(encoder(b, s), s * 4 + (b ^ i)) for b, s in PAIRS] for i in (0, 2)]
CORE_ROUTE = [(i, i ^ 1) for i in range(512)]


def one_hots():
    own = np.zeros((2, 2, 2, 3, 3, 3, 4, 5, 3, 4, 4, 2), np.float32)
    halo = np.zeros((2, 2, 2, 3, 3, 3, 4, 5, 4, 4, 3, 2), np.float32)
    for n in range(2):
        for par in range(2):
            for ky in range(3):
                t, yy = (n, 1) if ky == 0 else (n + 1, ky - 1)
                for kx in range(3):
                    r = 2 * par + kx
                    for c in range(4):
                        for plane, kz, z in ((0, 1, 0), (0, 2, 1), (1, 0, 1), (1, 1, 2), (1, 2, 3)):
                            own[plane, n, par, kz, ky, kx, c, r, t, c, z, yy] = 1
                        for plane, kz, z in ((0, 0, 1), (0, 1, 2), (0, 2, 3), (1, 0, 3)):
                            halo[plane, n, par, kz, ky, kx, c, r, t, c, z - 1, yy] = 1
    return own.reshape(8, 108, 480), halo.reshape(8, 108, 480)


def dot(a, b):
    return jnp.dot(a, b, preferred_element_type=F32)


def one_hot(rows, columns, hit):
    row = lax.broadcasted_iota(jnp.int32, (rows, columns), 0)
    column = lax.broadcasted_iota(jnp.int32, (rows, columns), 1)
    return jnp.where(hit(row, column), 1.0, 0.0).astype(BF)


def next_cell():
    return one_hot(128, 128, lambda q, to: q + 1 == to)


def split_phases(field_ref, out_ref, phases_ref):
    @pl.when(pl.program_id(0) == 0)
    def _():
        phases_ref[...] = one_hot(512, 512, lambda x, to: x == 4 * (to & 127) + (to >> 7))

    core = pl.program_id(0) & 1
    flips = 24 * (core ^ lax.axis_index("z_hi"))
    rows = dot(field_ref[...].reshape(256, 512), phases_ref[...])
    for k in range(32):
        out_ref[(k ^ (7 * ((k >> 3) & 1))) ^ flips, 0] = rows[8 * k : 8 * k + 8].astype(BF)


def mask_rows(region_ref, rows_ref, masked_ref, halo_ref):
    upper = one_hot(48, 64, lambda row, source: source == row + 2 * ((row * 43) >> 8) + 2)
    for pair in range(16):
        keep = region_ref[0, pair].astype(F32).astype(BF)
        rows = rows_ref[64 * pair : 64 * pair + 64, :] * keep
        masked_ref[64 * pair : 64 * pair + 64, :] = rows
        halo_ref[48 * pair : 48 * pair + 48, :] = dot(upper, rows).astype(BF)


def operand(first, parts):
    return jnp.concatenate([first] + [part[:, 128 * r : 128 * r + 128] for r in range(4) for part in parts], 0)


def silu(v):
    half = 0.5 * v
    return half + half * jnp.tanh(half)


def hidden_planes(lower, upper, rows, bias, low_plane):
    planes = (lower[0:rows], upper[0:rows] + lower[128 : 128 + rows], upper[128 : 128 + rows])
    values = [silu(plane + bias[0:rows]) for plane in planes]
    return [values[0] * low_plane] + values[1:]


def latent_row(second_ref, taps):
    both = dot(second_ref[...], taps)
    lane = lax.broadcasted_iota(jnp.int32, (128, 128), 1)
    return both[0:128] + jnp.where(lane == 0, 0.0, pltpu.roll(both[128:256], 1, 1))


def encode(place_ref, own_ref, zed_ref, why_ref, both_ref, own_kernel_ref, halo_kernel_ref, bias_ref, second_ref, out_ref, own_first, zed_first, hidden, latent):
    block, slab = place_ref[0], place_ref[1]
    shift = next_cell()
    own_first[0:64, :] = dot(why_ref[:, 384:512], shift).astype(BF)
    own_first[64:1088, :] = dot(own_ref[:, 384:512], shift).astype(BF)
    zed_first[0:48, :] = dot(both_ref[:, 384:512], shift).astype(BF)
    zed_first[48:816, :] = dot(zed_ref[:, 384:512], shift).astype(BF)
    bias = bias_ref[...]
    low_plane = jnp.where(slab == 0, 0.0, 1.0).astype(F32)
    low_row = jnp.where(block == 0, 0.0, 1.0).astype(F32)
    for p in range(17):
        rows, own_rows, zed_rows = 128, 96, 96
        own_w, zed_w = own_kernel_ref[...], halo_kernel_ref[...]
        if p == 16:
            rows, own_rows, zed_rows = 64, 64, 48
            own_w = jnp.concatenate([own_w[:, 96 * r : 96 * r + 64] for r in range(5)], 1)
            zed_w = jnp.concatenate([zed_w[:, 96 * r : 96 * r + 48] for r in range(5)], 1)
        if p == 0:
            own_parts, zed_parts = [why_ref[...], own_ref[0:32, :]], [both_ref[...], zed_ref[0:48, :]]
        else:
            own_parts = [own_ref[64 * p - 64 : 64 * p - 64 + own_rows, :]]
            zed_parts = [zed_ref[48 * p - 48 : 48 * p - 48 + zed_rows, :]]
        upper = dot(own_w, operand(own_first[64 * p : 64 * p + own_rows, :], own_parts))
        lower = dot(zed_w, operand(zed_first[48 * p : 48 * p + zed_rows, :], zed_parts))
        for kz, value in enumerate(hidden_planes(lower, upper, rows, bias, low_plane)):
            if p == 0:
                value = jnp.concatenate([value[0:64] * low_row, value[64:128]], 0)
            hidden[kz, 128 * p : 128 * p + rows, :] = value.astype(BF)
    for o in range(16):
        taps = jnp.concatenate([hidden[kz, 128 * o : 128 * o + 192, :] for kz in range(3)], 0)
        latent[:, o, :] = latent_row(second_ref, taps)
    for g in range(4):
        out_ref[(block & 2) ^ g] = latent[32 * g : 32 * g + 32].astype(BF)


def join_blocks(place_ref, a_ref, b_ref, other_ref, out_ref):
    group = place_ref[0]
    core = group & 1
    for i, ref in enumerate((a_ref, b_ref)):
        near = pl.multiple_of((group ^ (2 * i)) * 16, 16)
        out_ref[:, pl.ds(near, 16), :] = ref[core]
        far = pl.multiple_of((group ^ (2 * i + 1)) * 16, 16)
        out_ref[:, pl.ds(far, 16), :] = other_ref[i]


VMEM = pl.BlockSpec(memory_space=pltpu.VMEM)
SMEM = pl.BlockSpec(memory_space=pltpu.SMEM)
PARAMS = pltpu.CompilerParams(vmem_limit_bytes=32 * 1024 * 1024)


def body(field_rows, region, first_kernel, first_bias, second_kernel):
    own_hot, halo_hot = (jnp.asarray(a, BF) for a in one_hots())
    block = lax.axis_index("x_lo") * 2 + lax.axis_index("z_hi")
    inner = lax.axis_index("x_hi") * 2 + lax.axis_index("core")
    core = lax.axis_index("core")
    z_lo = lax.axis_index("z_lo") ^ (3 * (core ^ lax.axis_index("z_hi")))
    slab = inner * 32 + z_lo * 8 + (lax.axis_index("y") ^ (7 * (z_lo & 1)))
    place = jnp.stack([block, slab]).astype(jnp.int32)

    keep = lax.ppermute(region, FINE, REGION_ROUTE)
    split = pl.pallas_call(
        split_phases,
        grid=(4,),
        in_specs=[pl.BlockSpec((128, 2, 512), lambda i: (i, 0, 0))],
        out_specs=pl.BlockSpec((32, 1, 8, 512), lambda i: (0, i, 0, 0)),
        out_shape=jax.ShapeDtypeStruct((32, 4, 8, 512), BF),
        scratch_shapes=[pltpu.VMEM((512, 512), BF)],
        compiler_params=pltpu.CompilerParams(vmem_limit_bytes=60 * 1024 * 1024),
    )(field_rows.reshape(512, 2, 512))
    rows = lax.all_to_all(split.reshape(128, 8, 512), REGION, split_axis=0, concat_axis=0, tiled=True)
    taps = first_kernel.transpose(2, 3, 4, 1, 0).reshape(108, 32)
    own_kernel = jnp.einsum("kh,bkm->bhm", taps, own_hot, preferred_element_type=F32).astype(BF).reshape(256, 480)
    halo_kernel = jnp.einsum("kh,bkm->bhm", taps, halo_hot, preferred_element_type=F32).astype(BF).reshape(256, 480)
    bias = jnp.broadcast_to(jnp.tile(first_bias, 4)[:, None], (128, 128))
    second = second_kernel.transpose(0, 2, 3, 4, 1).reshape(128, 9, 3, 32)
    straight = second[:, :, 1:3].reshape(128, 576)
    earlier = jnp.pad(second[:, :, 0:1], ((0, 0), (0, 0), (1, 0), (0, 0))).reshape(128, 576)
    second = jnp.concatenate([straight, earlier], 0)

    rows, own_kernel, halo_kernel, bias, second = lax.optimization_barrier((rows, own_kernel, halo_kernel, bias, second))
    own, upper_rows = pl.pallas_call(
        mask_rows,
        in_specs=[SMEM, VMEM],
        out_specs=[VMEM, VMEM],
        out_shape=[jax.ShapeDtypeStruct((1024, 512), BF), jax.ShapeDtypeStruct((768, 512), BF)],
        compiler_params=PARAMS,
    )(keep, rows.reshape(1024, 512))
    zed = lax.ppermute(upper_rows, FINE, Z_ROUTE)
    why = lax.ppermute(own[960:1024], FINE, Y_ROUTE)
    both = lax.ppermute(upper_rows[720:768], FINE, ZY_ROUTE)
    pieces = pl.pallas_call(
        encode,
        in_specs=[SMEM] + [VMEM] * 8,
        out_specs=VMEM,
        out_shape=jax.ShapeDtypeStruct((4, 32, 16, 128), BF),
        scratch_shapes=[
            pltpu.VMEM((1088, 128), BF),
            pltpu.VMEM((816, 128), BF),
            pltpu.VMEM((3, 2112, 128), BF),
            pltpu.VMEM((128, 16, 128), F32),
        ],
        compiler_params=PARAMS,
    )(place, own, zed, why, both, own_kernel, halo_kernel, bias, second)
    a, b = (lax.ppermute(pieces[2 * i : 2 * i + 2], FINE, OUT_ROUTES[i]) for i in range(2))
    away = jnp.stack([lax.dynamic_index_in_dim(v, 1 - core, 0, keepdims=False) for v in (a, b)])
    other = lax.ppermute(away, FINE, CORE_ROUTE)
    joined = pl.pallas_call(
        join_blocks,
        in_specs=[SMEM] + [VMEM] * 3,
        out_specs=VMEM,
        out_shape=jax.ShapeDtypeStruct((32, 64, 128), BF),
        compiler_params=PARAMS,
    )(inner.astype(jnp.int32).reshape(1), a, b, other)
    return joined.reshape(32, 1, 64, 128)


def solution(mesh):
    fine = Mesh(mesh.devices.reshape(SHAPE), FINE)
    slab, chan = FINE[:4], FINE[4:]
    in_specs = (P(chan, None, slab, None), P(slab, chan), P(), P(), P())
    out_specs = P(chan, slab, None, None)
    return jax.shard_map(body, mesh=fine, in_specs=in_specs, out_specs=out_specs, check_vma=False)
```
